32 devices in a mesh: space: 8 (over z, x), member: 4 (over y, core).
Axes of the slice: x: 2, y: 2, z: 4, core: 2. Of those that a mesh axis runs over, the one named last changes fastest.
Arguments:
- fields: float32 [8, 16, 128, 256], P('member', 'space'), may hold values from -6 to 6
- velocity: float32 [16, 128, 256], P('space'), may hold values from 0.2 to 0.6
- building: int32 [16, 128, 256], P('space'), may hold values 0 or 1
- inflow_table: float32 [32, 128, 256], replicated, may hold values from -6 to 6
- inflow_index: int32 [8], P('member'), may hold values from 0 to 31
Outputs:
- fields_now: float32 [8, 16, 128, 256], P('member', 'space')
- r_factor: float32 [8, 8], replicated
The draws below stay inside these ranges and needn't reach their ends.
All inputs are finite; a program needn't handle non-finite values. No bound on the sum of `building` on one device may be relied on, other than what follows from the above.
Results may differ from the reference program's by a relative error of at most 0.0003.
Values may be sent and summed in bfloat16 or wider, within the bound.
A program may use at most 64 MiB of HBM per device.

```python
import math
import jax
import jax.numpy as jnp
from jax import lax

PY = 128
PZ = 256
PATTERNS = 32
STEPS = 2
MEMBERS = 8
NX = 16


def place_ends(drawn, rng, low, top_value):
    dims = drawn.shape
    place = [jax.random.randint(jax.random.fold_in(rng, axis), (), 0, dims[axis]) for axis in range(len(dims))]
    drawn = drawn.at[tuple(place)].set(low)
    longest = dims.index(max(dims))
    place[longest] = (place[longest] + 1) % dims[longest]
    return drawn.at[tuple(place)].set(top_value)


def shard_levels(key, extent, shards, smallest, largest):
    gain = 1.0
    for axis_at, shards_of in shards:
        heights = jax.random.uniform(jax.random.fold_in(jax.random.fold_in(key, 6), axis_at), (shards_of,), jnp.float32, smallest / len(shards), largest / len(shards))
        gain = gain * jnp.repeat(jnp.exp(heights), extent[axis_at] // shards_of).reshape((-1,) + (1,) * (len(extent) - 1 - axis_at))
    return gain


def centred(key, extent, deviation, most, cuts=(), held_as=jnp.bfloat16):
    drawn = jax.random.normal(key, extent, jnp.float32) * deviation
    if len(cuts) > 0:
        drawn = shard_levels(key, extent, cuts, -0.22, 0.18) * drawn
    return jnp.clip(drawn, min=-most, max=most).astype(held_as)


def setup_inputs(seed: int = 0) -> dict:
    seeds = jax.random.split(jax.random.key(seed), 6)
    return {
        "fields": centred(seeds[0], (MEMBERS, NX, PY, PZ), 1.0, 6.0, ((0, 4), (1, 8)), jnp.float32),
        "velocity": jnp.clip(jnp.exp(math.log(0.6) - 1.0986123 * jax.random.uniform(seeds[1], (NX, PY, PZ), jnp.float32) ** shard_levels(seeds[1], (NX, PY, PZ), ((0, 8),), -0.2, 0.2)), 0.2, 0.6),
        "building": place_ends((jax.random.randint(seeds[2], (NX, PY, PZ), 0, 8) < 1).astype(jnp.int32), jax.random.fold_in(seeds[2], 1), 0, 1),
        "inflow_table": centred(seeds[3], (PATTERNS, PY, PZ), 1.0, 6.0, (), jnp.float32),
        "inflow_index": place_ends(jax.random.randint(seeds[4], (MEMBERS,), 0, PATTERNS), jax.random.fold_in(seeds[4], 1), 0, PATTERNS - 1).astype(jnp.int32),
    }


kappa_rate = 0.05
shrink_weight = 0.1
contract_dims = (((1,), (1,)), ((), ()))

def advance(extended, fluid_cells, courant):
    upwind = extended[:, :-2]
    centre = extended[:, 1:-1]
    downwind = extended[:, 2:]
    in_plane = jnp.roll(centre, 1, 2) + jnp.roll(centre, -1, 2) + jnp.roll(centre, 1, 3) + jnp.roll(centre, -1, 3)
    return fluid_cells * (centre + courant * (upwind - centre) + kappa_rate * (upwind + downwind + in_plane - 6.0 * centre))

def reference(fields, velocity, building, inflow_table, inflow_index):
    fluid_cells = (1 - building).astype(jnp.float32)
    pattern_pick = (inflow_index[:, None] == jnp.arange(PATTERNS, dtype=jnp.int32)[None, :]).astype(jnp.float32)
    inflow_planes = jnp.dot(pattern_pick.astype(jnp.float32), inflow_table.reshape(PATTERNS, PY * PZ).astype(jnp.float32), precision=lax.Precision.HIGHEST, preferred_element_type=jnp.float32).reshape(MEMBERS, PY, PZ)

    def member_run(paired):
        field_now, inflow_plane = paired
        for sweep_index in range(STEPS):
            extended = jnp.concatenate([inflow_plane[None], field_now, jnp.zeros_like(inflow_plane)[None]], 0)[None]
            field_now = advance(extended, fluid_cells, velocity)[0]
        return field_now
    fields_now = lax.map(member_run, (fields, inflow_planes))
    ensemble_mean = jnp.sum(fields_now, 0) / MEMBERS
    anomaly = (fields_now - ensemble_mean).astype(jnp.bfloat16).reshape(MEMBERS, NX * PY * PZ)
    gram_full = lax.dot_general(anomaly.astype(jnp.float32), anomaly.astype(jnp.float32), contract_dims, preferred_element_type=jnp.float32) / (NX * PY * PZ)
    r_factor = jnp.linalg.cholesky(gram_full + shrink_weight * jnp.eye(MEMBERS, dtype=jnp.float32)).T
    return (fields_now, r_factor)
```

```python
import functools

import jax
import jax.numpy as jnp
from jax import lax
from jax.experimental import pallas as pl
from jax.experimental.pallas import tpu as pltpu
from jax.sharding import PartitionSpec as P

STEPS = 2

kappa_rate = 0.05
shrink_weight = 0.1
MESH = pl.DeviceIdType.MESH
HIGHEST = lax.Precision.HIGHEST


def kernel(
    slabs, groups, index, fields, velocity, building, table, out_f, out_r,
    f_v, v_v, b_v, t_v, coef_a, coef_b, coef_c, u1, u2, w_in, e_in, e_out,
    part_out, part_in, pair_rows, gram_a, gram_b,
    load_sem, save_sem, up_send, up_recv, down_send, down_recv,
    part_send, part_recv, a_send, a_recv, b_send, b_recv,
):
    mem, depth, rows, cols = f_v.shape
    members = mem * groups
    part_rows = part_out.shape[2]
    per_plane = groups // depth
    space = lax.axis_index("space")
    group = lax.axis_index("member")
    first = space == 0
    last = space == slabs - 1

    loads = [
        pltpu.make_async_copy(fields, f_v, load_sem.at[0]),
        pltpu.make_async_copy(velocity, v_v, load_sem.at[1]),
        pltpu.make_async_copy(building, b_v, load_sem.at[2]),
    ]
    for load in loads:
        load.start()
    table_load = pltpu.make_async_copy(table, t_v, load_sem.at[3])

    @pl.when(first)
    def _():
        table_load.start()

    barrier = pltpu.get_barrier_semaphore()
    for o in range(1, slabs):
        pl.semaphore_signal(
            barrier, inc=1, device_id=(lax.rem(space + o, slabs), group), device_id_type=MESH
        )
    for o in range(1, groups):
        pl.semaphore_signal(
            barrier, inc=1, device_id=(space, lax.rem(group + o, groups)), device_id_type=MESH
        )

    def up(step, m):
        source = fields if step == 0 else u1
        return pltpu.make_async_remote_copy(
            src_ref=source.at[m, depth - 1], dst_ref=w_in.at[step, m],
            send_sem=up_send.at[step, m], recv_sem=up_recv.at[step, m],
            device_id=(lax.rem(space + 1, slabs), group), device_id_type=MESH,
        )

    def down(step, m):
        return pltpu.make_async_remote_copy(
            src_ref=e_out.at[step, m], dst_ref=e_in.at[step, m],
            send_sem=down_send.at[step, m], recv_sem=down_recv.at[step, m],
            device_id=(lax.rem(space + slabs - 1, slabs), group), device_id_type=MESH,
        )

    loads[0].wait()
    for m in range(mem):
        e_out[0, m] = f_v[m, 0].astype(e_out.dtype)
    pl.semaphore_wait(barrier, slabs + groups - 2)

    @pl.when(jnp.logical_not(last))
    def _():
        for m in range(mem):
            up(0, m).start()

    @pl.when(jnp.logical_not(first))
    def _():
        for m in range(mem):
            down(0, m).start()

    @pl.when(last)
    def _():
        e_in[...] = jnp.zeros_like(e_in)

    loads[1].wait()
    loads[2].wait()
    for d in range(depth):
        fluid = (1 - b_v[d]).astype(jnp.float32)
        v = v_v[d]
        coef_a[d] = fluid * ((1.0 - 6.0 * kappa_rate) - v)
        coef_b[d] = fluid * (v + kappa_rate)
        coef_c[d] = fluid * kappa_rate

    @pl.when(first)
    def _():
        table_load.wait()
        for m in range(mem):
            plane = t_v[index[m]]
            for step in range(STEPS):
                w_in[step, m] = plane

    def part_copy(o):
        target = lax.rem(group + o, groups)
        return pltpu.make_async_remote_copy(
            src_ref=part_out.at[target], dst_ref=part_in.at[group],
            send_sem=part_send.at[o], recv_sem=part_recv.at[o],
            device_id=(space, target), device_id_type=MESH,
        )

    def finish(m, d):
        value = u2[m, d]
        pltpu.make_async_copy(u2.at[m, d], out_f.at[m, d], save_sem.at[m, d]).start()
        for i in range(per_plane):
            part_out[d * per_plane + i, m] = value[i * part_rows:(i + 1) * part_rows].astype(part_out.dtype)
        if m == mem - 1:
            for o in range(1, groups):
                @pl.when(lax.rem(group + o, groups) // per_plane == d)
                def _():
                    part_copy(o).start()

    old = f_v
    for step in range(STEPS):
        new = u1 if step == 0 else u2
        for m in range(mem):
            for d in range(depth):
                c = old[m, d]
                s = (
                    pltpu.roll(c, 1, 0) + pltpu.roll(c, rows - 1, 0)
                    + pltpu.roll(c, 1, 1) + pltpu.roll(c, cols - 1, 1)
                )
                if d < depth - 1:
                    s = s + old[m, d + 1]
                p = coef_a[d] * c + coef_c[d] * s
                if d > 0:
                    p = p + coef_b[d] * old[m, d - 1]
                new[m, d] = p
        for m in range(mem):
            @pl.when(jnp.logical_not(last))
            def _():
                down(step, m).wait_recv()

            new[m, depth - 1] += coef_c[depth - 1] * e_in[step, m].astype(jnp.float32)
            if step < STEPS - 1:
                @pl.when(jnp.logical_not(last))
                def _():
                    up(step + 1, m).start()
            else:
                finish(m, depth - 1)
        for m in range(mem):
            @pl.when(jnp.logical_not(first))
            def _():
                up(step, m).wait_recv()

            new[m, 0] += coef_b[0] * w_in[step, m]
            if step < STEPS - 1:
                e_out[step + 1, m] = new[m, 0].astype(e_out.dtype)

                @pl.when(jnp.logical_not(first))
                def _():
                    down(step + 1, m).start()
            else:
                finish(m, 0)
        old = new
    for d in range(1, depth - 1):
        for m in range(mem):
            finish(m, d)

    part_in[group] = part_out[group]
    for o in range(1, groups):
        part_copy(o).wait_recv()

    sums = {}
    for r in range(part_rows // 16):
        for l in range(cols // 128):
            us = [
                part_in[i // mem, i % mem, r * 16:(r + 1) * 16, l * 128:(l + 1) * 128].astype(jnp.float32)
                for i in range(members)
            ]
            mean = functools.reduce(lambda a, b: a + b, us) / members
            an = [(u - mean).astype(jnp.bfloat16).astype(jnp.float32) for u in us]
            for i in range(members):
                for j in range(i, members):
                    q = an[i] * an[j]
                    q = q[:8] + q[8:]
                    sums[i, j] = sums[i, j] + q if (i, j) in sums else q
    padded = pair_rows.shape[0]
    if padded > members * members:
        pair_rows[members * members:] = jnp.zeros((padded - members * members, 128), jnp.float32)
    for (i, j), q in sums.items():
        q = jnp.sum(q, 0, keepdims=True)
        pair_rows[i * members + j:i * members + j + 1] = q
        if i != j:
            pair_rows[j * members + i:j * members + i + 1] = q
    packed = lax.dot_general(
        jnp.ones((8, 128), jnp.float32), pair_rows[...], (((1,), (1,)), ((), ())),
        precision=HIGHEST, preferred_element_type=jnp.float32,
    )[0:1]

    def copy_a(o):
        return pltpu.make_async_remote_copy(
            src_ref=gram_a.at[group], dst_ref=gram_a.at[group],
            send_sem=a_send.at[o], recv_sem=a_recv.at[o],
            device_id=(space, lax.rem(group + o, groups)), device_id_type=MESH,
        )

    def copy_b(o):
        return pltpu.make_async_remote_copy(
            src_ref=gram_b.at[space], dst_ref=gram_b.at[space],
            send_sem=b_send.at[o], recv_sem=b_recv.at[o],
            device_id=(lax.rem(space + o, slabs), group), device_id_type=MESH,
        )

    gram_a[group] = packed
    for o in range(1, groups):
        copy_a(o).start()
    for o in range(1, groups):
        copy_a(o).wait_recv()
    gram_b[space] = jnp.sum(gram_a[...], 0)
    for o in range(1, slabs):
        copy_b(o).start()
    for o in range(1, slabs):
        copy_b(o).wait_recv()
    total = jnp.sum(gram_b[...], 0) / (slabs * depth * rows * cols)

    lane = lax.broadcasted_iota(jnp.int32, (members, padded), 1)
    row = lax.broadcasted_iota(jnp.int32, (members, padded), 0)
    spread = jnp.where(
        (lane >= row * members) & (lane < (row + 1) * members),
        jnp.broadcast_to(total, (members, padded)), 0.0,
    )
    source = lax.broadcasted_iota(jnp.int32, (padded, 128), 0)
    target = lax.broadcasted_iota(jnp.int32, (padded, 128), 1)
    fold = jnp.where(lax.rem(source, members) == target, 1.0, 0.0)
    gram = lax.dot_general(
        spread, fold, (((1,), (0,)), ((), ())), precision=HIGHEST, preferred_element_type=jnp.float32
    )
    row = lax.broadcasted_iota(jnp.int32, (members, 128), 0)
    lane = lax.broadcasted_iota(jnp.int32, (members, 128), 1)
    left = gram + jnp.where(row == lane, shrink_weight, 0.0)
    factor = jnp.zeros_like(left)
    for k in range(members):
        pivot = left[k:k + 1, k:k + 1]
        inverse = lax.rsqrt(pivot)
        inverse = inverse * (1.5 - 0.5 * pivot * inverse * inverse)
        line = left[k:k + 1] * inverse
        factor = jnp.where((row == k) & (lane >= k), line, factor)
        if k < members - 1:
            left = left - (left[:, k:k + 1] * inverse) * line
    out_r[...] = factor[:, :members]

    for m in range(mem):
        for d in range(depth):
            pltpu.make_async_copy(u2.at[m, d], out_f.at[m, d], save_sem.at[m, d]).wait()

    @pl.when(jnp.logical_not(last))
    def _():
        for step in range(STEPS):
            for m in range(mem):
                up(step, m).wait_send()

    @pl.when(jnp.logical_not(first))
    def _():
        for step in range(STEPS):
            for m in range(mem):
                down(step, m).wait_send()

    for o in range(1, groups):
        part_copy(o).wait_send()
        copy_a(o).wait_send()
    for o in range(1, slabs):
        copy_b(o).wait_send()


def local(slabs, groups, fields, velocity, building, inflow_table, inflow_index):
    mem, depth, rows, cols = fields.shape
    members = mem * groups
    padded = -(-members * members // 128) * 128
    f32, low = jnp.float32, jnp.bfloat16
    hbm = pl.BlockSpec(memory_space=pl.ANY)
    vmem, dma = pltpu.VMEM, pltpu.SemaphoreType.DMA
    slab = (depth, rows, cols)
    part = (groups, mem, depth * rows // groups, cols)
    return pl.pallas_call(
        functools.partial(kernel, slabs, groups),
        out_shape=(
            jax.ShapeDtypeStruct(fields.shape, f32),
            jax.ShapeDtypeStruct((members, members), f32),
        ),
        in_specs=[pl.BlockSpec(memory_space=pltpu.SMEM), hbm, hbm, hbm, hbm],
        out_specs=(hbm, pl.BlockSpec(memory_space=pltpu.VMEM)),
        scratch_shapes=[
            vmem(fields.shape, f32), vmem(slab, f32), vmem(slab, jnp.int32), vmem(inflow_table.shape, f32),
            vmem(slab, f32), vmem(slab, f32), vmem(slab, f32),
            vmem(fields.shape, f32), vmem(fields.shape, f32),
            vmem((STEPS, mem, rows, cols), f32),
            vmem((STEPS, mem, rows, cols), low), vmem((STEPS, mem, rows, cols), low),
            vmem(part, low), vmem(part, low), vmem((padded, 128), f32),
            vmem((groups, 1, padded), f32), vmem((slabs, 1, padded), f32),
            dma((4,)), dma((mem, depth)),
            dma((STEPS, mem)), dma((STEPS, mem)), dma((STEPS, mem)), dma((STEPS, mem)),
            dma((groups,)), dma((groups,)), dma((groups,)), dma((groups,)),
            dma((slabs,)), dma((slabs,)),
        ],
        compiler_params=pltpu.CompilerParams(
            collective_id=0, has_side_effects=True, vmem_limit_bytes=48 * 1024 * 1024
        ),
    )(inflow_index, fields, velocity, building, inflow_table)


def solution(mesh):
    placed = (
        P("member", "space", None, None),
        P("space", None, None),
        P("space", None, None),
        P(),
        P("member"),
    )
    return jax.shard_map(
        functools.partial(local, mesh.shape["space"], mesh.shape["member"]),
        mesh=mesh,
        in_specs=placed,
        out_specs=(P("member", "space", None, None), P()),
        check_vma=False,
    )
```

```python
import functools

import jax
import jax.numpy as jnp
from jax import lax
from jax.experimental import pallas as pl
from jax.experimental.pallas import tpu as pltpu
from jax.sharding import PartitionSpec as P

STEPS = 2

kappa_rate = 0.05
shrink_weight = 0.1
LEVELS = 32767.0
MESH = pl.DeviceIdType.MESH
HIGHEST = lax.Precision.HIGHEST


def kernel(
    slabs, groups, index, fields, velocity, building, table, out_f, out_r,
    f_v, v_v, b_v, t_v, coef_a, coef_b, coef_c, u1, u2, inflow, w_in, w_out, scale_in, scale_out, e_in, e_out,
    part_out, part_in, pair_rows, gram_a, gram_b,
    load_sem, save_sem, up_send, up_recv, scale_send, scale_recv, down_send, down_recv,
    part_send, part_recv, a_send, a_recv, b_send, b_recv,
):
    mem, depth, rows, cols = f_v.shape
    members = mem * groups
    part_rows = part_out.shape[2]
    per_plane = groups // depth
    space = lax.axis_index("space")
    group = lax.axis_index("member")
    first = space == 0
    last = space == slabs - 1

    loads = [
        pltpu.make_async_copy(fields, f_v, load_sem.at[0]),
        pltpu.make_async_copy(velocity, v_v, load_sem.at[1]),
        pltpu.make_async_copy(building, b_v, load_sem.at[2]),
    ]
    for load in loads:
        load.start()
    table_load = pltpu.make_async_copy(table, t_v, load_sem.at[3])

    @pl.when(first)
    def _():
        table_load.start()

    barrier = pltpu.get_barrier_semaphore()
    for o in range(1, slabs):
        pl.semaphore_signal(
            barrier, inc=1, device_id=(lax.rem(space + o, slabs), group), device_id_type=MESH
        )
    for o in range(1, groups):
        pl.semaphore_signal(
            barrier, inc=1, device_id=(space, lax.rem(group + o, groups)), device_id_type=MESH
        )

    def up(step, m):
        target = (lax.rem(space + 1, slabs), group)
        return (
            pltpu.make_async_remote_copy(
                src_ref=scale_out.at[step, m], dst_ref=scale_in.at[step, m],
                send_sem=scale_send.at[step, m], recv_sem=scale_recv.at[step, m],
                device_id=target, device_id_type=MESH,
            ),
            pltpu.make_async_remote_copy(
                src_ref=w_out.at[step, m], dst_ref=w_in.at[step, m],
                send_sem=up_send.at[step, m], recv_sem=up_recv.at[step, m],
                device_id=target, device_id_type=MESH,
            ),
        )

    def encode(step, m, plane):
        top = jnp.maximum(jnp.max(jnp.abs(plane), 0, keepdims=True), 1e-30)
        scale_out[step, m] = top * (1.0 / LEVELS)
        w_out[step, m] = jnp.round(plane * (LEVELS / top)).astype(jnp.int32).astype(jnp.int16)

    def down(step, m):
        return pltpu.make_async_remote_copy(
            src_ref=e_out.at[step, m], dst_ref=e_in.at[step, m],
            send_sem=down_send.at[step, m], recv_sem=down_recv.at[step, m],
            device_id=(lax.rem(space + slabs - 1, slabs), group), device_id_type=MESH,
        )

    loads[0].wait()
    for m in range(mem):
        encode(0, m, f_v[m, depth - 1])
        e_out[0, m] = f_v[m, 0].astype(e_out.dtype)
    pl.semaphore_wait(barrier, slabs + groups - 2)

    @pl.when(jnp.logical_not(last))
    def _():
        for m in range(mem):
            for copy in up(0, m):
                copy.start()

    @pl.when(jnp.logical_not(first))
    def _():
        for m in range(mem):
            down(0, m).start()

    @pl.when(last)
    def _():
        e_in[...] = jnp.zeros_like(e_in)

    loads[1].wait()
    loads[2].wait()
    for d in range(depth):
        fluid = (1 - b_v[d]).astype(jnp.float32)
        v = v_v[d]
        coef_a[d] = fluid * ((1.0 - 6.0 * kappa_rate) - v)
        coef_b[d] = fluid * (v + kappa_rate)
        coef_c[d] = fluid * kappa_rate

    @pl.when(first)
    def _():
        table_load.wait()
        for m in range(mem):
            inflow[m] = t_v[index[m]]

    def part_copy(o):
        target = lax.rem(group + o, groups)
        return pltpu.make_async_remote_copy(
            src_ref=part_out.at[target], dst_ref=part_in.at[group],
            send_sem=part_send.at[o], recv_sem=part_recv.at[o],
            device_id=(space, target), device_id_type=MESH,
        )

    def finish(m, d):
        value = u2[m, d]
        pltpu.make_async_copy(u2.at[m, d], out_f.at[m, d], save_sem.at[m, d]).start()
        for i in range(per_plane):
            part_out[d * per_plane + i, m] = value[i * part_rows:(i + 1) * part_rows].astype(part_out.dtype)
        if m == mem - 1:
            for o in range(1, groups):
                @pl.when(lax.rem(group + o, groups) // per_plane == d)
                def _():
                    part_copy(o).start()

    old = f_v
    for step in range(STEPS):
        new = u1 if step == 0 else u2
        for m in range(mem):
            for d in range(depth):
                c = old[m, d]
                s = (
                    pltpu.roll(c, 1, 0) + pltpu.roll(c, rows - 1, 0)
                    + pltpu.roll(c, 1, 1) + pltpu.roll(c, cols - 1, 1)
                )
                if d < depth - 1:
                    s = s + old[m, d + 1]
                p = coef_a[d] * c + coef_c[d] * s
                if d > 0:
                    p = p + coef_b[d] * old[m, d - 1]
                new[m, d] = p
        for m in range(mem):
            @pl.when(jnp.logical_not(last))
            def _():
                down(step, m).wait_recv()

            new[m, depth - 1] += coef_c[depth - 1] * e_in[step, m].astype(jnp.float32)
            if step < STEPS - 1:
                encode(step + 1, m, new[m, depth - 1])

                @pl.when(jnp.logical_not(last))
                def _():
                    for copy in up(step + 1, m):
                        copy.start()
            else:
                finish(m, depth - 1)
        for m in range(mem):
            @pl.when(jnp.logical_not(first))
            def _():
                for copy in up(step, m):
                    copy.wait_recv()
                inflow[m] = w_in[step, m].astype(jnp.int32).astype(jnp.float32) * scale_in[step, m]

            new[m, 0] += coef_b[0] * inflow[m]
            if step < STEPS - 1:
                e_out[step + 1, m] = new[m, 0].astype(e_out.dtype)

                @pl.when(jnp.logical_not(first))
                def _():
                    down(step + 1, m).start()
            else:
                finish(m, 0)
        old = new
    for d in range(1, depth - 1):
        for m in range(mem):
            finish(m, d)

    part_in[group] = part_out[group]
    for o in range(1, groups):
        part_copy(o).wait_recv()

    sums = {}
    for r in range(part_rows // 16):
        for l in range(cols // 128):
            us = [
                part_in[i // mem, i % mem, r * 16:(r + 1) * 16, l * 128:(l + 1) * 128].astype(jnp.float32)
                for i in range(members)
            ]
            mean = functools.reduce(lambda a, b: a + b, us) / members
            an = [(u - mean).astype(jnp.bfloat16).astype(jnp.float32) for u in us]
            for i in range(members):
                for j in range(i, members):
                    q = an[i] * an[j]
                    q = q[:8] + q[8:]
                    sums[i, j] = sums[i, j] + q if (i, j) in sums else q
    padded = pair_rows.shape[0]
    if padded > members * members:
        pair_rows[members * members:] = jnp.zeros((padded - members * members, 128), jnp.float32)
    for (i, j), q in sums.items():
        q = jnp.sum(q, 0, keepdims=True)
        pair_rows[i * members + j:i * members + j + 1] = q
        if i != j:
            pair_rows[j * members + i:j * members + i + 1] = q
    packed = lax.dot_general(
        jnp.ones((8, 128), jnp.float32), pair_rows[...], (((1,), (1,)), ((), ())),
        precision=HIGHEST, preferred_element_type=jnp.float32,
    )[0:1]

    def copy_a(o):
        return pltpu.make_async_remote_copy(
            src_ref=gram_a.at[group], dst_ref=gram_a.at[group],
            send_sem=a_send.at[o], recv_sem=a_recv.at[o],
            device_id=(space, lax.rem(group + o, groups)), device_id_type=MESH,
        )

    def copy_b(o):
        return pltpu.make_async_remote_copy(
            src_ref=gram_b.at[space], dst_ref=gram_b.at[space],
            send_sem=b_send.at[o], recv_sem=b_recv.at[o],
            device_id=(lax.rem(space + o, slabs), group), device_id_type=MESH,
        )

    gram_a[group] = packed
    for o in range(1, groups):
        copy_a(o).start()
    for o in range(1, groups):
        copy_a(o).wait_recv()
    gram_b[space] = jnp.sum(gram_a[...], 0)
    for o in range(1, slabs):
        copy_b(o).start()
    for o in range(1, slabs):
        copy_b(o).wait_recv()
    total = jnp.sum(gram_b[...], 0) / (slabs * depth * rows * cols)

    lane = lax.broadcasted_iota(jnp.int32, (members, padded), 1)
    row = lax.broadcasted_iota(jnp.int32, (members, padded), 0)
    spread = jnp.where(
        (lane >= row * members) & (lane < (row + 1) * members),
        jnp.broadcast_to(total, (members, padded)), 0.0,
    )
    source = lax.broadcasted_iota(jnp.int32, (padded, 128), 0)
    target = lax.broadcasted_iota(jnp.int32, (padded, 128), 1)
    fold = jnp.where(lax.rem(source, members) == target, 1.0, 0.0)
    gram = lax.dot_general(
        spread, fold, (((1,), (0,)), ((), ())), precision=HIGHEST, preferred_element_type=jnp.float32
    )
    row = lax.broadcasted_iota(jnp.int32, (members, 128), 0)
    lane = lax.broadcasted_iota(jnp.int32, (members, 128), 1)
    left = gram + jnp.where(row == lane, shrink_weight, 0.0)
    factor = jnp.zeros_like(left)
    for k in range(members):
        pivot = left[k:k + 1, k:k + 1]
        inverse = lax.rsqrt(pivot)
        inverse = inverse * (1.5 - 0.5 * pivot * inverse * inverse)
        line = left[k:k + 1] * inverse
        factor = jnp.where((row == k) & (lane >= k), line, factor)
        if k < members - 1:
            left = left - (left[:, k:k + 1] * inverse) * line
    out_r[...] = factor[:, :members]

    for m in range(mem):
        for d in range(depth):
            pltpu.make_async_copy(u2.at[m, d], out_f.at[m, d], save_sem.at[m, d]).wait()

    @pl.when(jnp.logical_not(last))
    def _():
        for step in range(STEPS):
            for m in range(mem):
                for copy in up(step, m):
                    copy.wait_send()

    @pl.when(jnp.logical_not(first))
    def _():
        for step in range(STEPS):
            for m in range(mem):
                down(step, m).wait_send()

    for o in range(1, groups):
        part_copy(o).wait_send()
        copy_a(o).wait_send()
    for o in range(1, slabs):
        copy_b(o).wait_send()


def local(slabs, groups, fields, velocity, building, inflow_table, inflow_index):
    mem, depth, rows, cols = fields.shape
    members = mem * groups
    padded = -(-members * members // 128) * 128
    f32, low = jnp.float32, jnp.bfloat16
    hbm = pl.BlockSpec(memory_space=pltpu.HBM)
    vmem, dma = pltpu.VMEM, pltpu.SemaphoreType.DMA
    slab = (depth, rows, cols)
    part = (groups, mem, depth * rows // groups, cols)
    return pl.pallas_call(
        functools.partial(kernel, slabs, groups),
        out_shape=(
            jax.ShapeDtypeStruct(fields.shape, f32),
            jax.ShapeDtypeStruct((members, members), f32),
        ),
        in_specs=[pl.BlockSpec(memory_space=pltpu.SMEM), hbm, hbm, hbm, hbm],
        out_specs=(hbm, pl.BlockSpec(memory_space=pltpu.VMEM)),
        scratch_shapes=[
            vmem(fields.shape, f32), vmem(slab, f32), vmem(slab, jnp.int32), vmem(inflow_table.shape, f32),
            vmem(slab, f32), vmem(slab, f32), vmem(slab, f32),
            vmem(fields.shape, f32), vmem(fields.shape, f32),
            vmem((mem, rows, cols), f32),
            vmem((STEPS, mem, rows, cols), jnp.int16), vmem((STEPS, mem, rows, cols), jnp.int16),
            vmem((STEPS, mem, 1, cols), f32), vmem((STEPS, mem, 1, cols), f32),
            vmem((STEPS, mem, rows, cols), low), vmem((STEPS, mem, rows, cols), low),
            vmem(part, low), vmem(part, low), vmem((padded, 128), f32),
            vmem((groups, 1, padded), f32), vmem((slabs, 1, padded), f32),
            dma((4,)), dma((mem, depth)),
            dma((STEPS, mem)), dma((STEPS, mem)), dma((STEPS, mem)), dma((STEPS, mem)),
            dma((STEPS, mem)), dma((STEPS, mem)),
            dma((groups,)), dma((groups,)), dma((groups,)), dma((groups,)),
            dma((slabs,)), dma((slabs,)),
        ],
        compiler_params=pltpu.CompilerParams(
            collective_id=0, has_side_effects=True, vmem_limit_bytes=64 * 1024 * 1024
        ),
    )(inflow_index, fields, velocity, building, inflow_table)


def solution(mesh):
    placed = (
        P("member", "space", None, None),
        P("space", None, None),
        P("space", None, None),
        P(),
        P("member"),
    )
    return jax.shard_map(
        functools.partial(local, mesh.shape["space"], mesh.shape["member"]),
        mesh=mesh,
        in_specs=placed,
        out_specs=(P("member", "space", None, None), P()),
        check_vma=False,
    )
```

```python
import functools

import jax
import jax.numpy as jnp
from jax import lax
from jax.experimental import pallas as pl
from jax.experimental.pallas import tpu as pltpu
from jax.sharding import PartitionSpec as P

STEPS = 2

kappa_rate = 0.05
shrink_weight = 0.1
LEVELS = 32767.0
MESH = pl.DeviceIdType.MESH
HIGHEST = lax.Precision.HIGHEST


def kernel(
    slabs, groups, index, fields, velocity, building, table, out_f, out_r,
    f_v, v_v, b_v, t_v, coef_a, coef_b, coef_c, u1, u2, inflow, w_in, w_out, scale_in, scale_out, e_in, e_out,
    part_out, part_in, pair_rows, gram_b,
    load_sem, save_sem, up_send, up_recv, scale_send, scale_recv, down_send, down_recv,
    part_send, part_recv, b_send, b_recv,
):
    mem, depth, rows, cols = f_v.shape
    members = mem * groups
    part_rows = part_out.shape[2]
    per_plane = groups // depth
    space = lax.axis_index("space")
    group = lax.axis_index("member")
    first = space == 0
    last = space == slabs - 1

    def partner(o):
        return lax.rem(space + o // groups, slabs), lax.rem(group + o % groups, groups)

    loads = [
        pltpu.make_async_copy(fields, f_v, load_sem.at[0]),
        pltpu.make_async_copy(velocity, v_v, load_sem.at[1]),
        pltpu.make_async_copy(building, b_v, load_sem.at[2]),
    ]
    for load in loads:
        load.start()
    table_load = pltpu.make_async_copy(table, t_v, load_sem.at[3])

    @pl.when(first)
    def _():
        table_load.start()

    barrier = pltpu.get_barrier_semaphore()
    for o in range(1, slabs * groups):
        pl.semaphore_signal(barrier, inc=1, device_id=partner(o), device_id_type=MESH)

    def up(step, m):
        target = (lax.rem(space + 1, slabs), group)
        return (
            pltpu.make_async_remote_copy(
                src_ref=scale_out.at[step, m], dst_ref=scale_in.at[step, m],
                send_sem=scale_send.at[step, m], recv_sem=scale_recv.at[step, m],
                device_id=target, device_id_type=MESH,
            ),
            pltpu.make_async_remote_copy(
                src_ref=w_out.at[step, m], dst_ref=w_in.at[step, m],
                send_sem=up_send.at[step, m], recv_sem=up_recv.at[step, m],
                device_id=target, device_id_type=MESH,
            ),
        )

    def encode(step, m, plane):
        top = jnp.maximum(jnp.max(jnp.abs(plane), 0, keepdims=True), 1e-30)
        scale_out[step, m] = top * (1.0 / LEVELS)
        w_out[step, m] = jnp.round(plane * (LEVELS / top)).astype(jnp.int32).astype(jnp.int16)

    def down(step, m):
        return pltpu.make_async_remote_copy(
            src_ref=e_out.at[step, m], dst_ref=e_in.at[step, m],
            send_sem=down_send.at[step, m], recv_sem=down_recv.at[step, m],
            device_id=(lax.rem(space + slabs - 1, slabs), group), device_id_type=MESH,
        )

    loads[0].wait()
    for m in range(mem):
        encode(0, m, f_v[m, depth - 1])
        e_out[0, m] = f_v[m, 0].astype(e_out.dtype)
    pl.semaphore_wait(barrier, slabs * groups - 1)

    @pl.when(jnp.logical_not(last))
    def _():
        for m in range(mem):
            for copy in up(0, m):
                copy.start()

    @pl.when(jnp.logical_not(first))
    def _():
        for m in range(mem):
            down(0, m).start()

    @pl.when(last)
    def _():
        e_in[...] = jnp.zeros_like(e_in)

    loads[1].wait()
    loads[2].wait()
    for d in range(depth):
        fluid = (1 - b_v[d]).astype(jnp.float32)
        v = v_v[d]
        coef_a[d] = fluid * ((1.0 - 6.0 * kappa_rate) - v)
        coef_b[d] = fluid * (v + kappa_rate)
        coef_c[d] = fluid * kappa_rate

    @pl.when(first)
    def _():
        table_load.wait()
        for m in range(mem):
            inflow[m] = t_v[index[m]]

    def part_copy(o):
        target = lax.rem(group + o, groups)
        return pltpu.make_async_remote_copy(
            src_ref=part_out.at[target], dst_ref=part_in.at[group],
            send_sem=part_send.at[o], recv_sem=part_recv.at[o],
            device_id=(space, target), device_id_type=MESH,
        )

    def finish(m, d):
        value = u2[m, d]
        pltpu.make_async_copy(u2.at[m, d], out_f.at[m, d], save_sem.at[m, d]).start()
        for i in range(per_plane):
            part_out[d * per_plane + i, m] = value[i * part_rows:(i + 1) * part_rows].astype(part_out.dtype)
        if m == mem - 1:
            for o in range(1, groups):
                @pl.when(lax.rem(group + o, groups) // per_plane == d)
                def _():
                    part_copy(o).start()

    old = f_v
    for step in range(STEPS):
        new = u1 if step == 0 else u2
        for m in range(mem):
            for d in range(depth):
                c = old[m, d]
                s = (
                    pltpu.roll(c, 1, 0) + pltpu.roll(c, rows - 1, 0)
                    + pltpu.roll(c, 1, 1) + pltpu.roll(c, cols - 1, 1)
                )
                if d < depth - 1:
                    s = s + old[m, d + 1]
                p = coef_a[d] * c + coef_c[d] * s
                if d > 0:
                    p = p + coef_b[d] * old[m, d - 1]
                new[m, d] = p
        for m in range(mem):
            @pl.when(jnp.logical_not(last))
            def _():
                down(step, m).wait_recv()

            new[m, depth - 1] += coef_c[depth - 1] * e_in[step, m].astype(jnp.float32)
            if step < STEPS - 1:
                encode(step + 1, m, new[m, depth - 1])

                @pl.when(jnp.logical_not(last))
                def _():
                    for copy in up(step + 1, m):
                        copy.start()
            else:
                finish(m, depth - 1)
        for m in range(mem):
            @pl.when(jnp.logical_not(first))
            def _():
                for copy in up(step, m):
                    copy.wait_recv()
                inflow[m] = w_in[step, m].astype(jnp.int32).astype(jnp.float32) * scale_in[step, m]

            new[m, 0] += coef_b[0] * inflow[m]
            if step < STEPS - 1:
                e_out[step + 1, m] = new[m, 0].astype(e_out.dtype)

                @pl.when(jnp.logical_not(first))
                def _():
                    down(step + 1, m).start()
            else:
                finish(m, 0)
        old = new
    for d in range(1, depth - 1):
        for m in range(mem):
            finish(m, d)

    part_in[group] = part_out[group]
    for o in range(1, groups):
        part_copy(o).wait_recv()

    sums = {}
    for r in range(part_rows // 16):
        for l in range(cols // 128):
            us = [
                part_in[i // mem, i % mem, r * 16:(r + 1) * 16, l * 128:(l + 1) * 128].astype(jnp.float32)
                for i in range(members)
            ]
            mean = functools.reduce(lambda a, b: a + b, us) / members
            an = [(u - mean).astype(jnp.bfloat16).astype(jnp.float32) for u in us]
            for i in range(members):
                for j in range(i, members):
                    q = an[i] * an[j]
                    q = q[:8] + q[8:]
                    sums[i, j] = sums[i, j] + q if (i, j) in sums else q
    padded = pair_rows.shape[0]
    if padded > members * members:
        pair_rows[members * members:] = jnp.zeros((padded - members * members, 128), jnp.float32)
    for (i, j), q in sums.items():
        q = jnp.sum(q, 0, keepdims=True)
        pair_rows[i * members + j:i * members + j + 1] = q
        if i != j:
            pair_rows[j * members + i:j * members + i + 1] = q
    packed = lax.dot_general(
        jnp.ones((8, 128), jnp.float32), pair_rows[...], (((1,), (1,)), ((), ())),
        precision=HIGHEST, preferred_element_type=jnp.float32,
    )[0:1]

    me = space * groups + group

    def copy_b(o):
        return pltpu.make_async_remote_copy(
            src_ref=gram_b.at[me], dst_ref=gram_b.at[me],
            send_sem=b_send.at[o], recv_sem=b_recv.at[o],
            device_id=partner(o), device_id_type=MESH,
        )

    gram_b[me] = packed
    for o in reversed(range(1, slabs * groups)):
        copy_b(o).start()
    for o in range(1, slabs * groups):
        copy_b(o).wait_recv()
    total = jnp.sum(gram_b[...], 0) / (slabs * depth * rows * cols)

    lane = lax.broadcasted_iota(jnp.int32, (members, padded), 1)
    row = lax.broadcasted_iota(jnp.int32, (members, padded), 0)
    spread = jnp.where(
        (lane >= row * members) & (lane < (row + 1) * members),
        jnp.broadcast_to(total, (members, padded)), 0.0,
    )
    source = lax.broadcasted_iota(jnp.int32, (padded, 128), 0)
    target = lax.broadcasted_iota(jnp.int32, (padded, 128), 1)
    fold = jnp.where(lax.rem(source, members) == target, 1.0, 0.0)
    gram = lax.dot_general(
        spread, fold, (((1,), (0,)), ((), ())), precision=HIGHEST, preferred_element_type=jnp.float32
    )
    row = lax.broadcasted_iota(jnp.int32, (members, 128), 0)
    lane = lax.broadcasted_iota(jnp.int32, (members, 128), 1)
    left = gram + jnp.where(row == lane, shrink_weight, 0.0)
    factor = jnp.zeros_like(left)
    for k in range(members):
        pivot = left[k:k + 1, k:k + 1]
        inverse = lax.rsqrt(pivot)
        inverse = inverse * (1.5 - 0.5 * pivot * inverse * inverse)
        line = left[k:k + 1] * inverse
        factor = jnp.where((row == k) & (lane >= k), line, factor)
        if k < members - 1:
            left = left - (left[:, k:k + 1] * inverse) * line
    out_r[...] = factor[:, :members]

    for m in range(mem):
        for d in range(depth):
            pltpu.make_async_copy(u2.at[m, d], out_f.at[m, d], save_sem.at[m, d]).wait()

    @pl.when(jnp.logical_not(last))
    def _():
        for step in range(STEPS):
            for m in range(mem):
                for copy in up(step, m):
                    copy.wait_send()

    @pl.when(jnp.logical_not(first))
    def _():
        for step in range(STEPS):
            for m in range(mem):
                down(step, m).wait_send()

    for o in range(1, groups):
        part_copy(o).wait_send()
    for o in range(1, slabs * groups):
        copy_b(o).wait_send()


def local(slabs, groups, fields, velocity, building, inflow_table, inflow_index):
    mem, depth, rows, cols = fields.shape
    members = mem * groups
    padded = -(-members * members // 128) * 128
    f32, low = jnp.float32, jnp.bfloat16
    hbm = pl.BlockSpec(memory_space=pltpu.HBM)
    vmem, dma = pltpu.VMEM, pltpu.SemaphoreType.DMA
    slab = (depth, rows, cols)
    part = (groups, mem, depth * rows // groups, cols)
    return pl.pallas_call(
        functools.partial(kernel, slabs, groups),
        out_shape=(
            jax.ShapeDtypeStruct(fields.shape, f32),
            jax.ShapeDtypeStruct((members, members), f32),
        ),
        in_specs=[pl.BlockSpec(memory_space=pltpu.SMEM), hbm, hbm, hbm, hbm],
        out_specs=(hbm, pl.BlockSpec(memory_space=pltpu.VMEM)),
        scratch_shapes=[
            vmem(fields.shape, f32), vmem(slab, f32), vmem(slab, jnp.int32), vmem(inflow_table.shape, f32),
            vmem(slab, f32), vmem(slab, f32), vmem(slab, f32),
            vmem(fields.shape, f32), vmem(fields.shape, f32),
            vmem((mem, rows, cols), f32),
            vmem((STEPS, mem, rows, cols), jnp.int16), vmem((STEPS, mem, rows, cols), jnp.int16),
            vmem((STEPS, mem, 1, cols), f32), vmem((STEPS, mem, 1, cols), f32),
            vmem((STEPS, mem, rows, cols), low), vmem((STEPS, mem, rows, cols), low),
            vmem(part, low), vmem(part, low), vmem((padded, 128), f32),
            vmem((slabs * groups, 1, padded), f32),
            dma((4,)), dma((mem, depth)),
            dma((STEPS, mem)), dma((STEPS, mem)), dma((STEPS, mem)), dma((STEPS, mem)),
            dma((STEPS, mem)), dma((STEPS, mem)),
            dma((groups,)), dma((groups,)),
            dma((slabs * groups,)), dma((slabs * groups,)),
        ],
        compiler_params=pltpu.CompilerParams(
            collective_id=0, has_side_effects=True, vmem_limit_bytes=64 * 1024 * 1024
        ),
    )(inflow_index, fields, velocity, building, inflow_table)


def solution(mesh):
    placed = (
        P("member", "space", None, None),
        P("space", None, None),
        P("space", None, None),
        P(),
        P("member"),
    )
    return jax.shard_map(
        functools.partial(local, mesh.shape["space"], mesh.shape["member"]),
        mesh=mesh,
        in_specs=placed,
        out_specs=(P("member", "space", None, None), P()),
        check_vma=False,
    )
```

```python
import functools

import jax
import jax.numpy as jnp
from jax import lax
from jax.experimental import pallas as pl
from jax.experimental.pallas import tpu as pltpu
from jax.sharding import PartitionSpec as P

STEPS = 2

kappa_rate = 0.05
shrink_weight = 0.1
LEVELS = 32767.0
MESH = pl.DeviceIdType.MESH
HIGHEST = lax.Precision.HIGHEST


def kernel(
    slabs, groups, index, fields, velocity, building, table, out_f, out_r,
    f_v, v_v, b_v, t_v, coef_a, coef_b, coef_c, u1, u2, inflow, w_in, w_out, scale_in, scale_out, e_in, e_out,
    part_out, part_in, pair_rows, gram_b,
    load_sem, save_sem, up_send, up_recv, scale_send, scale_recv, down_send, down_recv,
    part_send, part_recv, b_send, b_recv,
):
    mem, depth, rows, cols = f_v.shape
    members = mem * groups
    part_rows = part_out.shape[2]
    per_plane = groups // depth
    space = lax.axis_index("space")
    group = lax.axis_index("member")
    first = space == 0
    last = space == slabs - 1

    def partner(o):
        return lax.rem(space + o // groups, slabs), lax.rem(group + o % groups, groups)

    loads = [
        pltpu.make_async_copy(fields, f_v, load_sem.at[0]),
        pltpu.make_async_copy(velocity, v_v, load_sem.at[1]),
        pltpu.make_async_copy(building, b_v, load_sem.at[2]),
    ]
    for load in loads:
        load.start()
    table_load = pltpu.make_async_copy(table, t_v, load_sem.at[3])

    @pl.when(first)
    def _():
        table_load.start()

    barrier = pltpu.get_barrier_semaphore()
    for o in range(1, slabs * groups):
        pl.semaphore_signal(barrier, inc=1, device_id=partner(o), device_id_type=MESH)

    def up(step, m):
        target = (lax.rem(space + 1, slabs), group)
        return (
            pltpu.make_async_remote_copy(
                src_ref=scale_out.at[step, m], dst_ref=scale_in.at[step, m],
                send_sem=scale_send.at[step, m], recv_sem=scale_recv.at[step, m],
                device_id=target, device_id_type=MESH,
            ),
            pltpu.make_async_remote_copy(
                src_ref=w_out.at[step, m], dst_ref=w_in.at[step, m],
                send_sem=up_send.at[step, m], recv_sem=up_recv.at[step, m],
                device_id=target, device_id_type=MESH,
            ),
        )

    def encode(step, m, plane):
        top = jnp.maximum(jnp.max(jnp.abs(plane), 0, keepdims=True), 1e-30)
        scale_out[step, m] = top * (1.0 / LEVELS)
        w_out[step, m] = jnp.round(plane * (LEVELS / top)).astype(jnp.int32).astype(jnp.int16)

    def down(step, m):
        return pltpu.make_async_remote_copy(
            src_ref=e_out.at[step, m], dst_ref=e_in.at[step, m],
            send_sem=down_send.at[step, m], recv_sem=down_recv.at[step, m],
            device_id=(lax.rem(space + slabs - 1, slabs), group), device_id_type=MESH,
        )

    loads[0].wait()
    for m in range(mem):
        encode(0, m, f_v[m, depth - 1])
        e_out[0, m] = f_v[m, 0].astype(e_out.dtype)
    pl.semaphore_wait(barrier, slabs * groups - 1)

    @pl.when(jnp.logical_not(last))
    def _():
        for m in range(mem):
            for copy in up(0, m):
                copy.start()

    @pl.when(jnp.logical_not(first))
    def _():
        for m in range(mem):
            down(0, m).start()

    @pl.when(last)
    def _():
        e_in[...] = jnp.zeros_like(e_in)

    loads[1].wait()
    loads[2].wait()
    for d in range(depth):
        fluid = (1 - b_v[d]).astype(jnp.float32)
        v = v_v[d]
        coef_a[d] = fluid * ((1.0 - 6.0 * kappa_rate) - v)
        coef_b[d] = fluid * (v + kappa_rate)
        coef_c[d] = fluid * kappa_rate

    @pl.when(first)
    def _():
        table_load.wait()
        for m in range(mem):
            inflow[m] = t_v[index[m]]

    def part_copy(o, m):
        target = lax.rem(group + o, groups)
        return pltpu.make_async_remote_copy(
            src_ref=part_out.at[target, m], dst_ref=part_in.at[group, m],
            send_sem=part_send.at[o, m], recv_sem=part_recv.at[o, m],
            device_id=(space, target), device_id_type=MESH,
        )

    def finish(m, d):
        value = u2[m, d]
        pltpu.make_async_copy(u2.at[m, d], out_f.at[m, d], save_sem.at[m, d]).start()
        for i in range(per_plane):
            part_out[d * per_plane + i, m] = value[i * part_rows:(i + 1) * part_rows].astype(part_out.dtype)
        for o in range(1, groups):
            @pl.when(lax.rem(group + o, groups) // per_plane == d)
            def _():
                part_copy(o, m).start()

    old = f_v
    for step in range(STEPS):
        new = u1 if step == 0 else u2
        for m in range(mem):
            for d in range(depth):
                c = old[m, d]
                s = (
                    pltpu.roll(c, 1, 0) + pltpu.roll(c, rows - 1, 0)
                    + pltpu.roll(c, 1, 1) + pltpu.roll(c, cols - 1, 1)
                )
                if d < depth - 1:
                    s = s + old[m, d + 1]
                p = coef_a[d] * c + coef_c[d] * s
                if d > 0:
                    p = p + coef_b[d] * old[m, d - 1]
                new[m, d] = p
        for m in range(mem):
            @pl.when(jnp.logical_not(last))
            def _():
                down(step, m).wait_recv()

            new[m, depth - 1] += coef_c[depth - 1] * e_in[step, m].astype(jnp.float32)
            if step < STEPS - 1:
                encode(step + 1, m, new[m, depth - 1])

                @pl.when(jnp.logical_not(last))
                def _():
                    for copy in up(step + 1, m):
                        copy.start()
            else:
                finish(m, depth - 1)
        for m in range(mem):
            @pl.when(jnp.logical_not(first))
            def _():
                for copy in up(step, m):
                    copy.wait_recv()
                inflow[m] = w_in[step, m].astype(jnp.int32).astype(jnp.float32) * scale_in[step, m]

            new[m, 0] += coef_b[0] * inflow[m]
            if step < STEPS - 1:
                e_out[step + 1, m] = new[m, 0].astype(e_out.dtype)

                @pl.when(jnp.logical_not(first))
                def _():
                    down(step + 1, m).start()
            else:
                finish(m, 0)
        old = new
    for d in range(1, depth - 1):
        for m in range(mem):
            finish(m, d)

    part_in[group] = part_out[group]
    for o in range(1, groups):
        for m in range(mem):
            part_copy(o, m).wait_recv()

    sums = {}
    for r in range(part_rows // 16):
        for l in range(cols // 128):
            us = [
                part_in[i // mem, i % mem, r * 16:(r + 1) * 16, l * 128:(l + 1) * 128].astype(jnp.float32)
                for i in range(members)
            ]
            mean = functools.reduce(lambda a, b: a + b, us) / members
            an = [(u - mean).astype(jnp.bfloat16).astype(jnp.float32) for u in us]
            for i in range(members):
                for j in range(i, members):
                    q = an[i] * an[j]
                    q = q[:8] + q[8:]
                    sums[i, j] = sums[i, j] + q if (i, j) in sums else q
    padded = pair_rows.shape[0]
    if padded > members * members:
        pair_rows[members * members:] = jnp.zeros((padded - members * members, 128), jnp.float32)
    for (i, j), q in sums.items():
        q = jnp.sum(q, 0, keepdims=True)
        pair_rows[i * members + j:i * members + j + 1] = q
        if i != j:
            pair_rows[j * members + i:j * members + i + 1] = q
    packed = lax.dot_general(
        jnp.ones((8, 128), jnp.float32), pair_rows[...], (((1,), (1,)), ((), ())),
        precision=HIGHEST, preferred_element_type=jnp.float32,
    )[0:1]

    me = space * groups + group

    def copy_b(o):
        return pltpu.make_async_remote_copy(
            src_ref=gram_b.at[me], dst_ref=gram_b.at[me],
            send_sem=b_send.at[o], recv_sem=b_recv.at[o],
            device_id=partner(o), device_id_type=MESH,
        )

    gram_b[me] = packed
    for o in reversed(range(1, slabs * groups)):
        copy_b(o).start()
    for o in range(1, slabs * groups):
        copy_b(o).wait_recv()
    total = jnp.sum(gram_b[...], 0) / (slabs * depth * rows * cols)

    lane = lax.broadcasted_iota(jnp.int32, (members, padded), 1)
    row = lax.broadcasted_iota(jnp.int32, (members, padded), 0)
    spread = jnp.where(
        (lane >= row * members) & (lane < (row + 1) * members),
        jnp.broadcast_to(total, (members, padded)), 0.0,
    )
    source = lax.broadcasted_iota(jnp.int32, (padded, 128), 0)
    target = lax.broadcasted_iota(jnp.int32, (padded, 128), 1)
    fold = jnp.where(lax.rem(source, members) == target, 1.0, 0.0)
    gram = lax.dot_general(
        spread, fold, (((1,), (0,)), ((), ())), precision=HIGHEST, preferred_element_type=jnp.float32
    )
    row = lax.broadcasted_iota(jnp.int32, (members, 128), 0)
    lane = lax.broadcasted_iota(jnp.int32, (members, 128), 1)
    left = gram + jnp.where(row == lane, shrink_weight, 0.0)
    factor = jnp.zeros_like(left)
    for k in range(members):
        pivot = left[k:k + 1, k:k + 1]
        inverse = lax.rsqrt(pivot)
        inverse = inverse * (1.5 - 0.5 * pivot * inverse * inverse)
        line = left[k:k + 1] * inverse
        factor = jnp.where((row == k) & (lane >= k), line, factor)
        if k < members - 1:
            left = left - (left[:, k:k + 1] * inverse) * line
    out_r[...] = factor[:, :members]

    for m in range(mem):
        for d in range(depth):
            pltpu.make_async_copy(u2.at[m, d], out_f.at[m, d], save_sem.at[m, d]).wait()

    @pl.when(jnp.logical_not(last))
    def _():
        for step in range(STEPS):
            for m in range(mem):
                for copy in up(step, m):
                    copy.wait_send()

    @pl.when(jnp.logical_not(first))
    def _():
        for step in range(STEPS):
            for m in range(mem):
                down(step, m).wait_send()

    for o in range(1, groups):
        for m in range(mem):
            part_copy(o, m).wait_send()
    for o in range(1, slabs * groups):
        copy_b(o).wait_send()


def local(slabs, groups, fields, velocity, building, inflow_table, inflow_index):
    mem, depth, rows, cols = fields.shape
    members = mem * groups
    padded = -(-members * members // 128) * 128
    f32, low = jnp.float32, jnp.bfloat16
    hbm = pl.BlockSpec(memory_space=pltpu.HBM)
    vmem, dma = pltpu.VMEM, pltpu.SemaphoreType.DMA
    slab = (depth, rows, cols)
    part = (groups, mem, depth * rows // groups, cols)
    return pl.pallas_call(
        functools.partial(kernel, slabs, groups),
        out_shape=(
            jax.ShapeDtypeStruct(fields.shape, f32),
            jax.ShapeDtypeStruct((members, members), f32),
        ),
        in_specs=[pl.BlockSpec(memory_space=pltpu.SMEM), hbm, hbm, hbm, hbm],
        out_specs=(hbm, pl.BlockSpec(memory_space=pltpu.VMEM)),
        scratch_shapes=[
            vmem(fields.shape, f32), vmem(slab, f32), vmem(slab, jnp.int32), vmem(inflow_table.shape, f32),
            vmem(slab, f32), vmem(slab, f32), vmem(slab, f32),
            vmem(fields.shape, f32), vmem(fields.shape, f32),
            vmem((mem, rows, cols), f32),
            vmem((STEPS, mem, rows, cols), jnp.int16), vmem((STEPS, mem, rows, cols), jnp.int16),
            vmem((STEPS, mem, 1, cols), f32), vmem((STEPS, mem, 1, cols), f32),
            vmem((STEPS, mem, rows, cols), low), vmem((STEPS, mem, rows, cols), low),
            vmem(part, low), vmem(part, low), vmem((padded, 128), f32),
            vmem((slabs * groups, 1, padded), f32),
            dma((4,)), dma((mem, depth)),
            dma((STEPS, mem)), dma((STEPS, mem)), dma((STEPS, mem)), dma((STEPS, mem)),
            dma((STEPS, mem)), dma((STEPS, mem)),
            dma((groups, mem)), dma((groups, mem)),
            dma((slabs * groups,)), dma((slabs * groups,)),
        ],
        compiler_params=pltpu.CompilerParams(
            collective_id=0, has_side_effects=True, vmem_limit_bytes=64 * 1024 * 1024
        ),
    )(inflow_index, fields, velocity, building, inflow_table)


def solution(mesh):
    placed = (
        P("member", "space", None, None),
        P("space", None, None),
        P("space", None, None),
        P(),
        P("member"),
    )
    return jax.shard_map(
        functools.partial(local, mesh.shape["space"], mesh.shape["member"]),
        mesh=mesh,
        in_specs=placed,
        out_specs=(P("member", "space", None, None), P()),
        check_vma=False,
    )
```

```python
import functools

import jax
import jax.numpy as jnp
from jax import lax
from jax.experimental import pallas as pl
from jax.experimental.pallas import tpu as pltpu
from jax.sharding import PartitionSpec as P

STEPS = 2

kappa_rate = 0.05
shrink_weight = 0.1
LEVELS = 32767.0
MESH = pl.DeviceIdType.MESH
HIGHEST = lax.Precision.HIGHEST


def kernel(
    slabs, groups, index, fields, velocity, building, table, out_f, out_r,
    f_v, v_v, b_v, t_v, coef_a, coef_b, coef_c, u1, u2, inflow, w_in, w_out, scale_in, scale_out, e_in, e_out,
    part_out, part_in, pair_rows, gram_b,
    load_sem, save_sem, up_send, up_recv, scale_send, scale_recv, down_send, down_recv,
    part_send, part_recv, b_send, b_recv,
):
    mem, depth, rows, cols = f_v.shape
    members = mem * groups
    part_rows = part_out.shape[2]
    per_plane = groups // depth
    space = lax.axis_index("space")
    group = lax.axis_index("member")
    first = space == 0
    last = space == slabs - 1

    def partner(o):
        return lax.rem(space + o // groups, slabs), lax.rem(group + o % groups, groups)

    loads = [
        pltpu.make_async_copy(fields, f_v, load_sem.at[0]),
        pltpu.make_async_copy(velocity, v_v, load_sem.at[1]),
        pltpu.make_async_copy(building, b_v, load_sem.at[2]),
    ]
    for load in loads:
        load.start()
    table_load = pltpu.make_async_copy(table, t_v, load_sem.at[3])

    @pl.when(first)
    def _():
        table_load.start()

    barrier = pltpu.get_barrier_semaphore()
    for o in range(1, slabs * groups):
        pl.semaphore_signal(barrier, inc=1, device_id=partner(o), device_id_type=MESH)

    def up(step, m):
        target = (lax.rem(space + 1, slabs), group)
        return (
            pltpu.make_async_remote_copy(
                src_ref=scale_out.at[step, m], dst_ref=scale_in.at[step, m],
                send_sem=scale_send.at[step, m], recv_sem=scale_recv.at[step, m],
                device_id=target, device_id_type=MESH,
            ),
            pltpu.make_async_remote_copy(
                src_ref=w_out.at[step, m], dst_ref=w_in.at[step, m],
                send_sem=up_send.at[step, m], recv_sem=up_recv.at[step, m],
                device_id=target, device_id_type=MESH,
            ),
        )

    def encode(step, m, plane):
        top = jnp.maximum(jnp.max(jnp.abs(plane), 0, keepdims=True), 1e-30)
        scale_out[step, m] = top * (1.0 / LEVELS)
        w_out[step, m] = jnp.round(plane * (LEVELS / top)).astype(jnp.int32).astype(jnp.int16)

    def down(step, m):
        return pltpu.make_async_remote_copy(
            src_ref=e_out.at[step, m], dst_ref=e_in.at[step, m],
            send_sem=down_send.at[step, m], recv_sem=down_recv.at[step, m],
            device_id=(lax.rem(space + slabs - 1, slabs), group), device_id_type=MESH,
        )

    loads[0].wait()
    for m in range(mem):
        encode(0, m, f_v[m, depth - 1])
        e_out[0, m] = f_v[m, 0].astype(e_out.dtype)
    pl.semaphore_wait(barrier, slabs * groups - 1)

    @pl.when(jnp.logical_not(first))
    def _():
        for m in range(mem):
            down(0, m).start()

    @pl.when(jnp.logical_not(last))
    def _():
        for m in range(mem):
            for copy in up(0, m):
                copy.start()

    @pl.when(last)
    def _():
        e_in[...] = jnp.zeros_like(e_in)

    loads[1].wait()
    loads[2].wait()
    for d in range(depth):
        fluid = (1 - b_v[d]).astype(jnp.float32)
        v = v_v[d]
        coef_a[d] = fluid * ((1.0 - 6.0 * kappa_rate) - v)
        coef_b[d] = fluid * (v + kappa_rate)
        coef_c[d] = fluid * kappa_rate

    @pl.when(first)
    def _():
        table_load.wait()
        for m in range(mem):
            inflow[m] = t_v[index[m]]

    def part_copy(o, m):
        target = lax.rem(group + o, groups)
        return pltpu.make_async_remote_copy(
            src_ref=part_out.at[target, m], dst_ref=part_in.at[group, m],
            send_sem=part_send.at[o, m], recv_sem=part_recv.at[o, m],
            device_id=(space, target), device_id_type=MESH,
        )

    def finish(m, d):
        value = u2[m, d]
        pltpu.make_async_copy(u2.at[m, d], out_f.at[m, d], save_sem.at[m, d]).start()
        for i in range(per_plane):
            part_out[d * per_plane + i, m] = value[i * part_rows:(i + 1) * part_rows].astype(part_out.dtype)
        for o in range(1, groups):
            @pl.when(lax.rem(group + o, groups) // per_plane == d)
            def _():
                part_copy(o, m).start()

    old = f_v
    for step in range(STEPS):
        new = u1 if step == 0 else u2
        for m in range(mem):
            for d in range(depth):
                c = old[m, d]
                s = (
                    pltpu.roll(c, 1, 0) + pltpu.roll(c, rows - 1, 0)
                    + pltpu.roll(c, 1, 1) + pltpu.roll(c, cols - 1, 1)
                )
                if d < depth - 1:
                    s = s + old[m, d + 1]
                p = coef_a[d] * c + coef_c[d] * s
                if d > 0:
                    p = p + coef_b[d] * old[m, d - 1]
                new[m, d] = p
        def top(step, new):
            for m in range(mem):
                @pl.when(jnp.logical_not(last))
                def _():
                    down(step, m).wait_recv()

                new[m, depth - 1] += coef_c[depth - 1] * e_in[step, m].astype(jnp.float32)
                if step < STEPS - 1:
                    encode(step + 1, m, new[m, depth - 1])

                    @pl.when(jnp.logical_not(last))
                    def _():
                        for copy in up(step + 1, m):
                            copy.start()
                else:
                    finish(m, depth - 1)

        def bottom(step, new):
            for m in range(mem):
                @pl.when(jnp.logical_not(first))
                def _():
                    for copy in up(step, m):
                        copy.wait_recv()
                    inflow[m] = w_in[step, m].astype(jnp.int32).astype(jnp.float32) * scale_in[step, m]

                new[m, 0] += coef_b[0] * inflow[m]
                if step < STEPS - 1:
                    e_out[step + 1, m] = new[m, 0].astype(e_out.dtype)

                    @pl.when(jnp.logical_not(first))
                    def _():
                        down(step + 1, m).start()
                else:
                    finish(m, 0)

        for edge in (top, bottom) if step < STEPS - 1 else (bottom, top):
            edge(step, new)
        old = new
    for d in range(1, depth - 1):
        for m in range(mem):
            finish(m, d)

    part_in[group] = part_out[group]
    for o in range(1, groups):
        for m in range(mem):
            part_copy(o, m).wait_recv()

    sums = {}
    for r in range(part_rows // 16):
        for l in range(cols // 128):
            us = [
                part_in[i // mem, i % mem, r * 16:(r + 1) * 16, l * 128:(l + 1) * 128].astype(jnp.float32)
                for i in range(members)
            ]
            mean = functools.reduce(lambda a, b: a + b, us) / members
            an = [(u - mean).astype(jnp.bfloat16).astype(jnp.float32) for u in us]
            for i in range(members):
                for j in range(i, members):
                    q = an[i] * an[j]
                    q = q[:8] + q[8:]
                    sums[i, j] = sums[i, j] + q if (i, j) in sums else q
    padded = pair_rows.shape[0]
    if padded > members * members:
        pair_rows[members * members:] = jnp.zeros((padded - members * members, 128), jnp.float32)
    for (i, j), q in sums.items():
        q = jnp.sum(q, 0, keepdims=True)
        pair_rows[i * members + j:i * members + j + 1] = q
        if i != j:
            pair_rows[j * members + i:j * members + i + 1] = q
    packed = lax.dot_general(
        jnp.ones((8, 128), jnp.float32), pair_rows[...], (((1,), (1,)), ((), ())),
        precision=HIGHEST, preferred_element_type=jnp.float32,
    )[0:1]

    me = space * groups + group

    def copy_b(o):
        return pltpu.make_async_remote_copy(
            src_ref=gram_b.at[me], dst_ref=gram_b.at[me],
            send_sem=b_send.at[o], recv_sem=b_recv.at[o],
            device_id=partner(o), device_id_type=MESH,
        )

    gram_b[me] = packed
    for o in reversed(range(1, slabs * groups)):
        copy_b(o).start()
    for o in range(1, slabs * groups):
        copy_b(o).wait_recv()
    total = jnp.sum(gram_b[...], 0) / (slabs * depth * rows * cols)

    lane = lax.broadcasted_iota(jnp.int32, (members, padded), 1)
    row = lax.broadcasted_iota(jnp.int32, (members, padded), 0)
    spread = jnp.where(
        (lane >= row * members) & (lane < (row + 1) * members),
        jnp.broadcast_to(total, (members, padded)), 0.0,
    )
    source = lax.broadcasted_iota(jnp.int32, (padded, 128), 0)
    target = lax.broadcasted_iota(jnp.int32, (padded, 128), 1)
    fold = jnp.where(lax.rem(source, members) == target, 1.0, 0.0)
    gram = lax.dot_general(
        spread, fold, (((1,), (0,)), ((), ())), precision=HIGHEST, preferred_element_type=jnp.float32
    )
    row = lax.broadcasted_iota(jnp.int32, (members, 128), 0)
    lane = lax.broadcasted_iota(jnp.int32, (members, 128), 1)
    left = gram + jnp.where(row == lane, shrink_weight, 0.0)
    factor = jnp.zeros_like(left)
    for k in range(members):
        pivot = left[k:k + 1, k:k + 1]
        inverse = lax.rsqrt(pivot)
        inverse = inverse * (1.5 - 0.5 * pivot * inverse * inverse)
        line = left[k:k + 1] * inverse
        factor = jnp.where((row == k) & (lane >= k), line, factor)
        if k < members - 1:
            left = left - (left[:, k:k + 1] * inverse) * line
    out_r[...] = factor[:, :members]

    for m in range(mem):
        for d in range(depth):
            pltpu.make_async_copy(u2.at[m, d], out_f.at[m, d], save_sem.at[m, d]).wait()

    @pl.when(jnp.logical_not(last))
    def _():
        for step in range(STEPS):
            for m in range(mem):
                for copy in up(step, m):
                    copy.wait_send()

    @pl.when(jnp.logical_not(first))
    def _():
        for step in range(STEPS):
            for m in range(mem):
                down(step, m).wait_send()

    for o in range(1, groups):
        for m in range(mem):
            part_copy(o, m).wait_send()
    for o in range(1, slabs * groups):
        copy_b(o).wait_send()


def local(slabs, groups, fields, velocity, building, inflow_table, inflow_index):
    mem, depth, rows, cols = fields.shape
    members = mem * groups
    padded = -(-members * members // 128) * 128
    f32, low = jnp.float32, jnp.bfloat16
    hbm = pl.BlockSpec(memory_space=pltpu.HBM)
    vmem, dma = pltpu.VMEM, pltpu.SemaphoreType.DMA
    slab = (depth, rows, cols)
    part = (groups, mem, depth * rows // groups, cols)
    return pl.pallas_call(
        functools.partial(kernel, slabs, groups),
        out_shape=(
            jax.ShapeDtypeStruct(fields.shape, f32),
            jax.ShapeDtypeStruct((members, members), f32),
        ),
        in_specs=[pl.BlockSpec(memory_space=pltpu.SMEM), hbm, hbm, hbm, hbm],
        out_specs=(hbm, pl.BlockSpec(memory_space=pltpu.VMEM)),
        scratch_shapes=[
            vmem(fields.shape, f32), vmem(slab, f32), vmem(slab, jnp.int32), vmem(inflow_table.shape, f32),
            vmem(slab, f32), vmem(slab, f32), vmem(slab, f32),
            vmem(fields.shape, f32), vmem(fields.shape, f32),
            vmem((mem, rows, cols), f32),
            vmem((STEPS, mem, rows, cols), jnp.int16), vmem((STEPS, mem, rows, cols), jnp.int16),
            vmem((STEPS, mem, 1, cols), f32), vmem((STEPS, mem, 1, cols), f32),
            vmem((STEPS, mem, rows, cols), low), vmem((STEPS, mem, rows, cols), low),
            vmem(part, low), vmem(part, low), vmem((padded, 128), f32),
            vmem((slabs * groups, 1, padded), f32),
            dma((4,)), dma((mem, depth)),
            dma((STEPS, mem)), dma((STEPS, mem)), dma((STEPS, mem)), dma((STEPS, mem)),
            dma((STEPS, mem)), dma((STEPS, mem)),
            dma((groups, mem)), dma((groups, mem)),
            dma((slabs * groups,)), dma((slabs * groups,)),
        ],
        compiler_params=pltpu.CompilerParams(
            collective_id=0, has_side_effects=True, vmem_limit_bytes=64 * 1024 * 1024
        ),
    )(inflow_index, fields, velocity, building, inflow_table)


def solution(mesh):
    placed = (
        P("member", "space", None, None),
        P("space", None, None),
        P("space", None, None),
        P(),
        P("member"),
    )
    return jax.shard_map(
        functools.partial(local, mesh.shape["space"], mesh.shape["member"]),
        mesh=mesh,
        in_specs=placed,
        out_specs=(P("member", "space", None, None), P()),
        check_vma=False,
    )
```
